1024 devices in a mesh: section: 16 (over x_hi, y), tp: 8 (over z), dp: 8 (over x_lo, core).
Axes of the slice: x: 8 (x_hi: 2, x_lo: 4; x = x_hi * 4 + x_lo), y: 8, z: 8, core: 2. Of those that a mesh axis runs over, the one named last changes fastest.
Arguments:
- stash: bfloat16 [16, 8, 320, 48, 384], P('section', 'dp', None, 'tp'), may hold values from -24 to 24
- grad_out: bfloat16 [16, 8, 320, 6144], P('section', 'dp', None, 'tp'), may hold values from -6 to 6
- doc_lengths: int32 [16, 8, 8], P('section', 'dp'), may hold values from 1 to 160, 320 in all within a row
Outputs:
- qkv_grad: bfloat16 [16, 8, 320, 48, 384], P('section', 'dp', None, 'tp')
- bias_grad: float32 [16, 48, 384], P('section', 'tp')
The draws below stay inside these ranges and needn't reach their ends.
Inputs may be any that keep to these rules, and one draw needn't show every extreme that they name: `doc_lengths`: the 8 lengths of one micro-batch sum to 320, and in each micro-batch one of them is exactly 160.
All inputs are finite; a program needn't handle non-finite values.
Results may differ from the reference program's by a relative error of at most 0.012.
Values may be sent and summed in bfloat16 or wider, within the bound.
A program may use at most 32 MiB of HBM per device.

```python
import math
import jax
import jax.numpy as jnp
import numpy as np
from jax import lax

HEADS = 48
HEAD_DIM = 128
L = 320
DOCS = 8
QKV = 384
PIPE = 16
MB = 8
N_DP = 8


def draw_stash(key, part):
    shape = (PIPE, MB, L, HEADS, QKV)
    normal_draw = jax.random.normal(key, shape, jnp.float32)
    return jnp.clip(normal_draw, -24.0, 24.0).astype(jnp.bfloat16)


def steps_of(stream_key, dims, split, least, top_value):
    def one(axis_at, parts):
        draws = jax.random.uniform(jax.random.fold_in(jax.random.fold_in(stream_key, 6), axis_at), (parts,), jnp.float32, least / len(split), top_value / len(split))
        return jnp.repeat(jnp.exp(draws), dims[axis_at] // parts).reshape((-1,) + (1,) * (len(dims) - axis_at - 1))

    level = one(*split[0])
    for cut in split[1:]:
        level = level * one(*cut)
    return level


def length_profile(count, total, reach, slope):
    portions = [(1 << 20) // math.isqrt(rank ** slope) + 1 for rank in range(2, count + 1)]
    rest, holding = total - reach - (count - 1), [1] * (count - 1)
    while rest > 0:
        free = [i for i in range(count - 1) if holding[i] < reach]
        mass, remaining = sum([portions[i] for i in free]), rest
        for i in free:
            extra = min(reach - holding[i], max(1, remaining * portions[i] // mass), rest)
            holding[i] = holding[i] + extra
            rest = rest - extra
    return np.array([reach] + holding)


def ragged_sizes(stream_key, count, total, most, lean):
    if count == 2:
        one = jax.random.randint(stream_key, (), max(1, total - most), min(most, total - 1) + 1)
        return jnp.stack([one, total - one])
    sizes = jnp.asarray(length_profile(count, total, most, lean), jnp.int32)
    pairs = (count - 1) // 2
    source_of, taker = sizes[1:1 + 2 * pairs:2], sizes[2:2 + 2 * pairs:2]
    margin = jnp.minimum(source_of - 1, most - taker)
    moved = jax.random.randint(jax.random.fold_in(stream_key, 1), (pairs,), 0, 1 << 20) % (margin + 1)
    sizes = sizes.at[1:1 + 2 * pairs:2].set(source_of - moved).at[2:2 + 2 * pairs:2].set(taker + moved)
    return sizes[jax.random.permutation(jax.random.fold_in(stream_key, 2), count)]


def centred(own_key, extent, scale, reach, shards=(), held_as=jnp.bfloat16):
    factor_of = steps_of(own_key, extent, shards, -0.22, 0.18) if shards else 1.0
    result = jax.random.normal(own_key, extent, jnp.float32) * scale * factor_of
    return jnp.minimum(jnp.maximum(result, -reach), reach).astype(held_as)


def setup_inputs(seed: int = 0) -> dict:
    keys = jax.random.split(jax.random.key(seed), 4)
    stash = draw_stash(jax.random.fold_in(keys[3], 71), 0)
    grad_out = centred(keys[1], (PIPE, MB, L, HEADS * HEAD_DIM), 1.0, 6.0, ((0, 16), (1, 8), (3, 8)))
    doc_lengths = jax.vmap(lambda own: ragged_sizes(own, DOCS, L, L // 2, 2))(jax.random.split(keys[2], PIPE * MB)).reshape((PIPE, MB, DOCS)).astype(jnp.int32)
    return dict(stash=stash, grad_out=grad_out, doc_lengths=doc_lengths)


def segment_of(lengths, row_count):
    doc_ends = jnp.cumsum(lengths.astype(jnp.int32))
    position = jnp.arange(row_count, dtype=jnp.int32)
    return lax.optimization_barrier(jnp.sum((position[:, None] >= doc_ends[None, :]).astype(jnp.int32), axis=1))

def attention_grads(packed, grad_rows, lengths):
    row_count, head_count, pack_width = packed.shape
    head_size = pack_width // 3
    inv_root = 1.0 / math.sqrt(head_size)
    queries = packed[:, :, :head_size].astype(jnp.float32)
    keys_in = packed[:, :, head_size:2 * head_size].astype(jnp.float32)
    values_in = packed[:, :, 2 * head_size:].astype(jnp.float32)
    grad_heads = grad_rows.reshape(row_count, head_count, head_size).astype(jnp.float32)
    segment = segment_of(lengths, row_count)
    position = jnp.arange(row_count, dtype=jnp.int32)
    allowed = (segment[:, None] == segment[None, :]) & (position[None, :] <= position[:, None])
    scores = jnp.einsum('qhd,khd->hqk', queries, keys_in) * inv_root
    masked = jnp.where(allowed[None], scores, -jnp.inf)
    row_top = lax.optimization_barrier(jnp.max(masked, axis=-1, keepdims=True))
    raised = jnp.exp(masked - row_top)
    attn_prob = raised / lax.optimization_barrier(jnp.sum(raised, axis=-1, keepdims=True))
    prob_low = attn_prob.astype(jnp.bfloat16).astype(jnp.float32)
    attn_out = jnp.einsum('hqk,khd->qhd', prob_low, values_in)
    row_dot = jnp.einsum('qhd,qhd->hq', grad_heads, attn_out)
    prob_grad = jnp.einsum('qhd,khd->hqk', grad_heads, values_in)
    score_grad = attn_prob * (prob_grad - row_dot[:, :, None]) * inv_root
    score_low = score_grad.astype(jnp.bfloat16).astype(jnp.float32)
    query_grad = jnp.einsum('hqk,khd->qhd', score_low, keys_in)
    key_grad = jnp.einsum('hqk,qhd->khd', score_low, queries)
    value_grad = jnp.einsum('hqk,qhd->khd', prob_low, grad_heads)
    return jnp.concatenate([query_grad, key_grad, value_grad], axis=-1)

def one_block(inputs):
    packed, grad_rows, lengths = inputs
    grads = attention_grads(packed, grad_rows, lengths)
    return (grads.astype(jnp.bfloat16), lax.optimization_barrier(jnp.sum(grads, axis=0)))

def reference(stash, grad_out, doc_lengths):
    owned = stash[::-1]
    flat_stash = owned.reshape(PIPE * MB, L, HEADS, QKV)
    flat_grad = grad_out.reshape(PIPE * MB, L, HEADS * HEAD_DIM)
    flat_len = doc_lengths.reshape(PIPE * MB, DOCS)
    grads_low, bias_terms = lax.map(one_block, (flat_stash, flat_grad, flat_len))
    qkv_grad = grads_low.reshape(PIPE, MB, L, HEADS, QKV)
    bias_grad = lax.optimization_barrier(jnp.sum(bias_terms.reshape(PIPE, MB, HEADS, QKV), axis=1)) / N_DP
    return (qkv_grad, bias_grad)
```

```python
import functools
import math

import jax
import jax.numpy as jnp
from jax import lax
from jax.experimental import pallas as pl
from jax.experimental.pallas import tpu as pltpu
from jax.sharding import PartitionSpec as P

MESH = pl.DeviceIdType.MESH
CUTS = 4


def partners(sections, x_parts, y_parts):
    section = lax.axis_index("section")
    x_hi, y = section // y_parts, section % y_parts
    over = (1 - x_hi) * y_parts + y
    flipped = x_hi * y_parts + (y_parts - 1 - y)
    return over, flipped


def allowed_bias(ends_ref, docs, rows):
    query = lax.broadcasted_iota(jnp.int32, (1, rows), 1)
    start = jnp.zeros((1, rows), jnp.int32)
    end = jnp.int32(0)
    for d in range(docs):
        end = end + ends_ref[d]
        start = jnp.where(query >= end, end, start)
    key = lax.broadcasted_iota(jnp.int32, (rows, rows), 0)
    query = lax.broadcasted_iota(jnp.int32, (rows, rows), 1)
    return jnp.where((key <= query) & (key >= start), 0.0, -jnp.inf).astype(jnp.float32)


def head_grads(q, k, v, g, mask):
    inv_root = 1.0 / math.sqrt(q.shape[-1])
    nt = (((1,), (1,)), ((), ()))
    tn = (((0,), (0,)), ((), ()))
    nn = (((1,), (0,)), ((), ()))
    dot = functools.partial(lax.dot_general, preferred_element_type=jnp.float32)
    scores = dot(k, q, nt) * (inv_root * math.log2(math.e)) + mask
    raised = jnp.exp2(scores - jnp.max(scores, axis=0, keepdims=True))
    prob = raised * (1.0 / jnp.sum(raised, axis=0, keepdims=True))
    prob_low = prob.astype(jnp.bfloat16)
    prob_grad = dot(v, g, nt)
    row_dot = jnp.sum(prob_low.astype(jnp.float32) * prob_grad, axis=0, keepdims=True)
    score_low = (prob * (prob_grad - row_dot) * inv_root).astype(jnp.bfloat16)
    return dot(score_low, k, tn), dot(score_low, q, nn), dot(prob_low, g, nn)


def kernel(shape, stash, grad_out, lengths, made, bias_out, relay, land, g_all, mask, bias_part, bias_all,
           s1, r1, s2, r2, g_sem, bias_send, bias_recv):
    sections, x_parts, y_parts, replicas = shape
    heads, rows, width = land.shape
    size = width // 3
    cut = rows // CUTS
    over, flipped = partners(sections, x_parts, y_parts)
    me = lax.axis_index("dp")
    peers = [lax.rem(me + n, replicas) for n in range(1, replicas)]

    barrier = pltpu.get_barrier_semaphore()
    for to in (over, flipped):
        pl.semaphore_signal(barrier, inc=1, device_id={"section": to}, device_id_type=MESH)
    for to in peers:
        pl.semaphore_signal(barrier, inc=1, device_id={"dp": to}, device_id_type=MESH)
    g_copy = pltpu.make_async_copy(grad_out, g_all, g_sem)
    g_copy.start()
    pl.semaphore_wait(barrier, 2 + len(peers))

    def piece(ref, h, n):
        return ref.at[h, pl.ds(n * cut, cut)]

    def hop(src, dst, send, recv, h, n, to):
        at = h * CUTS + n
        return pltpu.make_async_remote_copy(
            src_ref=piece(src, h, n), dst_ref=piece(dst, h, n), send_sem=send.at[at],
            recv_sem=recv.at[at], device_id={"section": to}, device_id_type=MESH)

    def first(h, n):
        return hop(stash, relay, s1, r1, h, n, over if n % 2 else flipped)

    def second(h, n):
        return hop(relay, land, s2, r2, h, n, flipped if n % 2 else over)

    @pl.loop(0, heads)
    def _(h):
        for n in range(CUTS):
            first(h, n).start()

    mask[...] = allowed_bias(lengths, lengths.shape[0], rows)

    @pl.loop(0, heads)
    def _(h):
        for n in range(CUTS):
            first(h, n).wait_recv()
            second(h, n).start()

    g_copy.wait()

    @pl.loop(0, heads)
    def _(h):
        for n in range(CUTS):
            second(h, n).wait_recv()
        q = land[h, :, 0:size]
        k = land[h, :, size:2 * size]
        v = land[h, :, 2 * size:]
        g = g_all[:, pl.ds(pl.multiple_of(h * size, size), size)]
        for n, part in enumerate(head_grads(q, k, v, g, mask[...])):
            made[h, :, n * size:(n + 1) * size] = part.astype(made.dtype)
            bias_part[h, :, n * size:(n + 1) * size] = jnp.sum(part.reshape(-1, 8, size), axis=0)

    def bias_copy(n):
        return pltpu.make_async_remote_copy(
            src_ref=bias_all.at[me], dst_ref=bias_all.at[me], send_sem=bias_send.at[n],
            recv_sem=bias_recv.at[n], device_id={"dp": peers[n]}, device_id_type=MESH)

    for h in range(heads):
        bias_all[me, h:h + 1] = jnp.sum(bias_part[h], axis=0, keepdims=True)
    for n in range(len(peers)):
        bias_copy(n).start()

    @pl.loop(0, heads)
    def _(h):
        for n in range(CUTS):
            first(h, n).wait_send()
            second(h, n).wait_send()

    for n in range(len(peers)):
        bias_copy(n).wait()
    total = bias_all[0]
    for n in range(1, replicas):
        total = total + bias_all[n]
    total = total / replicas
    for h in range(heads):
        bias_out[h] = total[h:h + 1]


def solution(mesh):
    sections, replicas = mesh.shape["section"], mesh.shape["dp"]
    x_parts = 2
    shape = (sections, x_parts, sections // x_parts, replicas)

    def body(stash, grad_out, doc_lengths):
        _, _, rows, heads, width = stash.shape
        held = jnp.transpose(stash[0, 0], (1, 0, 2))
        pieces = heads * CUTS
        dma = pltpu.SemaphoreType.DMA
        made, bias = pl.pallas_call(
            functools.partial(kernel, shape),
            out_shape=(jax.ShapeDtypeStruct(held.shape, held.dtype),
                       jax.ShapeDtypeStruct((heads, 1, width), jnp.float32)),
            in_specs=[pl.BlockSpec(memory_space=pltpu.HBM), pl.BlockSpec(memory_space=pltpu.HBM),
                      pl.BlockSpec(memory_space=pltpu.SMEM)],
            out_specs=(pl.BlockSpec(memory_space=pltpu.VMEM), pl.BlockSpec(memory_space=pltpu.VMEM)),
            scratch_shapes=[
                pltpu.VMEM(held.shape, held.dtype),
                pltpu.VMEM(held.shape, held.dtype),
                pltpu.VMEM(grad_out.shape[2:], grad_out.dtype),
                pltpu.VMEM((rows, rows), jnp.float32),
                pltpu.VMEM((heads, 8, width), jnp.float32),
                pltpu.VMEM((replicas, heads, width), jnp.float32),
                dma((pieces,)), dma((pieces,)), dma((pieces,)), dma((pieces,)),
                dma, dma((replicas - 1,)), dma((replicas - 1,)),
            ],
            compiler_params=pltpu.CompilerParams(
                collective_id=0, has_side_effects=True, vmem_limit_bytes=40 << 20),
            name="mirror_attention_grads",
        )(held, grad_out[0, 0], doc_lengths[0, 0])
        return jnp.transpose(made, (1, 0, 2))[None, None], jnp.transpose(bias, (1, 0, 2))

    in_specs = (
        P("section", "dp", None, "tp", None),
        P("section", "dp", None, "tp"),
        P("section", "dp", None),
    )
    out_specs = (P("section", "dp", None, "tp", None), P("section", "tp", None))
    return jax.shard_map(body, mesh=mesh, in_specs=in_specs, out_specs=out_specs, check_vma=False)
```

```python
import functools
import math

import jax
import jax.numpy as jnp
from jax import lax
from jax.experimental import pallas as pl
from jax.experimental.pallas import tpu as pltpu
from jax.sharding import PartitionSpec as P

MESH = pl.DeviceIdType.MESH
CUTS = 4
LIMIT = 56 << 20


def partners(sections, x_parts, y_parts):
    section = lax.axis_index("section")
    x_hi, y = section // y_parts, section % y_parts
    over = (1 - x_hi) * y_parts + y
    flipped = x_hi * y_parts + (y_parts - 1 - y)
    return over, flipped


def allowed_bias(ends_ref, docs, rows):
    query = lax.broadcasted_iota(jnp.int32, (1, rows), 1)
    start = jnp.zeros((1, rows), jnp.int32)
    end = jnp.int32(0)
    for d in range(docs):
        end = end + ends_ref[d]
        start = jnp.where(query >= end, end, start)
    key = lax.broadcasted_iota(jnp.int32, (rows, rows), 0)
    query = lax.broadcasted_iota(jnp.int32, (rows, rows), 1)
    return jnp.where((key <= query) & (key >= start), 0.0, -jnp.inf).astype(jnp.float32)


def head_grads(q, k, v, g, mask):
    inv_root = 1.0 / math.sqrt(q.shape[-1])
    nt = (((1,), (1,)), ((), ()))
    tn = (((0,), (0,)), ((), ()))
    nn = (((1,), (0,)), ((), ()))
    dot = functools.partial(lax.dot_general, preferred_element_type=jnp.float32)
    scores = dot(k, q, nt) * (inv_root * math.log2(math.e)) + mask
    raised = jnp.exp2(scores - jnp.max(scores, axis=0, keepdims=True))
    prob = raised * (1.0 / jnp.sum(raised, axis=0, keepdims=True))
    prob_low = prob.astype(jnp.bfloat16)
    prob_grad = dot(v, g, nt)
    row_dot = jnp.sum(prob_low.astype(jnp.float32) * prob_grad, axis=0, keepdims=True)
    score_low = (prob * (prob_grad - row_dot) * inv_root).astype(jnp.bfloat16)
    return dot(score_low, k, tn), dot(score_low, q, nn), dot(prob_low, g, nn)


def exchange_kernel(shape, stash, grad_out, lengths, out, bias_local, own, relay, land, made, g_all, mask,
                    bias_part, s1, r1, s2, r2, own_sem, out_sem, g_sem):
    sections, x_parts, y_parts = shape
    heads, rows, width = land.shape
    size = width // 3
    cut = rows // CUTS
    over, flipped = partners(sections, x_parts, y_parts)

    barrier = pltpu.get_barrier_semaphore()
    for to in (over, flipped):
        pl.semaphore_signal(barrier, inc=1, device_id={"section": to}, device_id_type=MESH)

    def load(h):
        return pltpu.make_async_copy(stash.at[h], own.at[h], own_sem.at[h])

    def store(h):
        return pltpu.make_async_copy(made.at[h], out.at[h], out_sem.at[h])

    @pl.loop(0, heads)
    def _(h):
        load(h).start()

    g_copy = pltpu.make_async_copy(grad_out, g_all, g_sem)
    g_copy.start()
    pl.semaphore_wait(barrier, 2)

    def piece(ref, h, n):
        return ref.at[h, pl.ds(n * cut, cut)]

    def hop(src, dst, send, recv, h, n, to):
        at = h * CUTS + n
        return pltpu.make_async_remote_copy(
            src_ref=piece(src, h, n), dst_ref=piece(dst, h, n), send_sem=send.at[at],
            recv_sem=recv.at[at], device_id={"section": to}, device_id_type=MESH)

    def first(h, n):
        return hop(own, relay, s1, r1, h, n, over if n % 2 else flipped)

    def second(h, n):
        return hop(relay, land, s2, r2, h, n, flipped if n % 2 else over)

    @pl.loop(0, heads)
    def _(h):
        load(h).wait()
        for n in range(CUTS):
            first(h, n).start()

    mask[...] = allowed_bias(lengths, lengths.shape[0], rows)

    @pl.loop(0, heads)
    def _(h):
        for n in range(CUTS):
            first(h, n).wait_recv()
            second(h, n).start()

    g_copy.wait()

    @pl.loop(0, heads)
    def _(h):
        for n in range(CUTS):
            second(h, n).wait_recv()
        q = land[h, :, 0:size]
        k = land[h, :, size:2 * size]
        v = land[h, :, 2 * size:]
        g = g_all[:, pl.ds(pl.multiple_of(h * size, size), size)]
        for n, part in enumerate(head_grads(q, k, v, g, mask[...])):
            made[h, :, n * size:(n + 1) * size] = part.astype(made.dtype)
            bias_part[h, :, n * size:(n + 1) * size] = jnp.sum(part.reshape(-1, 8, size), axis=0)
        store(h).start()

    for h in range(heads):
        bias_local[h:h + 1] = jnp.sum(bias_part[h], axis=0, keepdims=True)

    @pl.loop(0, heads)
    def _(h):
        for n in range(CUTS):
            first(h, n).wait_send()
            second(h, n).wait_send()
        store(h).wait()


def bias_kernel(replicas, bias_local, bias_out, bias_all, bias_send, bias_recv, own_sem):
    heads = bias_local.shape[0]
    me = lax.axis_index("dp")
    peers = [lax.rem(me + n, replicas) for n in range(1, replicas)]
    barrier = pltpu.get_barrier_semaphore()
    for to in peers:
        pl.semaphore_signal(barrier, inc=1, device_id={"dp": to}, device_id_type=MESH)
    own = pltpu.make_async_copy(bias_local, bias_all.at[me], own_sem)
    own.start()
    pl.semaphore_wait(barrier, len(peers))
    copies = [
        pltpu.make_async_remote_copy(
            src_ref=bias_local, dst_ref=bias_all.at[me], send_sem=bias_send.at[n],
            recv_sem=bias_recv.at[n], device_id={"dp": to}, device_id_type=MESH)
        for n, to in enumerate(peers)
    ]
    for copy in copies:
        copy.start()
    for copy in [own, *copies]:
        copy.wait()
    total = bias_all[0]
    for n in range(1, replicas):
        total = total + bias_all[n]
    total = total / replicas
    for h in range(heads):
        bias_out[h] = total[h:h + 1]


def solution(mesh):
    sections, replicas = mesh.shape["section"], mesh.shape["dp"]
    x_parts = 2
    shape = (sections, x_parts, sections // x_parts)
    vmem, hbm = pl.BlockSpec(memory_space=pltpu.VMEM), pl.BlockSpec(memory_space=pltpu.HBM)

    def body(stash, grad_out, doc_lengths):
        _, _, rows, heads, width = stash.shape
        held = jnp.transpose(stash[0, 0], (1, 0, 2))
        pieces = heads * CUTS
        dma = pltpu.SemaphoreType.DMA
        made, bias_local = pl.pallas_call(
            functools.partial(exchange_kernel, shape),
            out_shape=(jax.ShapeDtypeStruct(held.shape, held.dtype),
                       jax.ShapeDtypeStruct((heads, width), jnp.float32)),
            in_specs=[hbm, hbm, pl.BlockSpec(memory_space=pltpu.SMEM)],
            out_specs=(hbm, vmem),
            scratch_shapes=[
                pltpu.VMEM(held.shape, held.dtype),
                pltpu.VMEM(held.shape, held.dtype),
                pltpu.VMEM(held.shape, held.dtype),
                pltpu.VMEM(held.shape, held.dtype),
                pltpu.VMEM(grad_out.shape[2:], grad_out.dtype),
                pltpu.VMEM((rows, rows), jnp.float32),
                pltpu.VMEM((heads, 8, width), jnp.float32),
                dma((pieces,)), dma((pieces,)), dma((pieces,)), dma((pieces,)),
                dma((heads,)), dma((heads,)), dma,
            ],
            compiler_params=pltpu.CompilerParams(
                collective_id=0, has_side_effects=True, vmem_limit_bytes=LIMIT),
            name="mirror_attention_grads",
        )(held, grad_out[0, 0], doc_lengths[0, 0])
        bias = pl.pallas_call(
            functools.partial(bias_kernel, replicas),
            out_shape=jax.ShapeDtypeStruct((heads, 1, width), jnp.float32),
            in_specs=[hbm],
            out_specs=vmem,
            scratch_shapes=[
                pltpu.VMEM((replicas, heads, width), jnp.float32),
                dma((replicas - 1,)), dma((replicas - 1,)), dma,
            ],
            compiler_params=pltpu.CompilerParams(collective_id=1, has_side_effects=True),
            name="bias_mean",
        )(bias_local)
        return jnp.transpose(made, (1, 0, 2))[None, None], jnp.transpose(bias, (1, 0, 2))

    in_specs = (
        P("section", "dp", None, "tp", None),
        P("section", "dp", None, "tp"),
        P("section", "dp", None),
    )
    out_specs = (P("section", "dp", None, "tp", None), P("section", "tp", None))
    return jax.shard_map(body, mesh=mesh, in_specs=in_specs, out_specs=out_specs, check_vma=False)
```

```python
import functools
import math

import jax
import jax.numpy as jnp
from jax import lax
from jax.experimental import pallas as pl
from jax.experimental.pallas import tpu as pltpu
from jax.sharding import PartitionSpec as P

MESH = pl.DeviceIdType.MESH
CUTS = 4
SHIFT = 1
LIMIT = 52 << 20


def partners(sections, x_parts, y_parts):
    section = lax.axis_index("section")
    x_hi, y = section // y_parts, section % y_parts
    over = (1 - x_hi) * y_parts + y
    flipped = x_hi * y_parts + (y_parts - 1 - y)
    return over, flipped


def allowed_bias(ends_ref, docs, rows):
    query = lax.broadcasted_iota(jnp.int32, (1, rows), 1)
    start = jnp.zeros((1, rows), jnp.int32)
    end = jnp.int32(0)
    for d in range(docs):
        end = end + ends_ref[d]
        start = jnp.where(query >= end, end, start)
    key = lax.broadcasted_iota(jnp.int32, (rows, rows), 0)
    query = lax.broadcasted_iota(jnp.int32, (rows, rows), 1)
    return jnp.where((key <= query) & (key >= start), 0.0, -jnp.inf).astype(jnp.float32)


def head_grads(q, k, v, g, mask):
    inv_root = 1.0 / math.sqrt(q.shape[-1])
    nt = (((1,), (1,)), ((), ()))
    tn = (((0,), (0,)), ((), ()))
    nn = (((1,), (0,)), ((), ()))
    dot = functools.partial(lax.dot_general, preferred_element_type=jnp.float32)
    scores = dot(k, q, nt) * (inv_root * math.log2(math.e)) + mask
    raised = jnp.exp2(scores - jnp.max(scores, axis=0, keepdims=True))
    prob = raised * (1.0 / jnp.sum(raised, axis=0, keepdims=True))
    prob_low = prob.astype(jnp.bfloat16)
    prob_grad = dot(v, g, nt)
    row_dot = jnp.sum(prob_low.astype(jnp.float32) * prob_grad, axis=0, keepdims=True)
    score_low = (prob * (prob_grad - row_dot) * inv_root).astype(jnp.bfloat16)
    return dot(score_low, k, tn), dot(score_low, q, nn), dot(prob_low, g, nn)


def kernel(shape, stash, grad_out, lengths, made, bias_out, own, from_over, from_flipped, land, g_all, mask,
           bias_part, bias_all, s1, r_over, r_flipped, s_over, s_flipped, r2, own_sem, g_sem, bias_send, bias_recv):
    sections, x_parts, y_parts, replicas = shape
    heads, rows, width = land.shape
    size = width // 3
    cut = rows // CUTS
    over, flipped = partners(sections, x_parts, y_parts)
    me = lax.axis_index("dp")
    peers = [lax.rem(me + n, replicas) for n in range(1, replicas)]

    def load(h):
        return pltpu.make_async_copy(stash.at[h], own.at[h], own_sem.at[h])

    barrier = pltpu.get_barrier_semaphore()

    def greet(**to):
        pl.semaphore_signal(barrier, inc=1, device_id=to, device_id_type=MESH)

    greet(section=over)
    greet(section=flipped)

    for to in peers:
        greet(dp=to)

    @pl.loop(0, heads)
    def _(h):
        load(h).start()

    g_copy = pltpu.make_async_copy(grad_out, g_all, g_sem)
    g_copy.start()
    pl.semaphore_wait(barrier, 2 + len(peers))

    def hop(src, dst, send, recv, h, n, to):
        at, rows_at = h * CUTS + n, pl.ds(n * cut, cut)
        return pltpu.make_async_remote_copy(
            src_ref=src.at[h, rows_at], dst_ref=dst.at[h, rows_at], send_sem=send.at[at],
            recv_sem=recv.at[at], device_id={"section": to}, device_id_type=MESH)

    def x_first(h, n):
        return hop(own, from_over, s1, r_over, h, n, over)

    def y_first(h, n):
        return hop(own, from_flipped, s1, r_flipped, h, n, flipped)

    def y_second(h, n):
        return hop(from_over, land, s_over, r2, h, n, flipped)

    def x_second(h, n):
        return hop(from_flipped, land, s_flipped, r2, h, n, over)

    y = lax.axis_index("section") % y_parts
    first_plane = lax.axis_index("tp") == 0
    low = first_plane & (y == 0)
    high = first_plane & (y == y_parts - 1)

    def goes_x_first(h, n, low, high):
        moved = h < SHIFT
        if n == 1:
            return jnp.logical_not(low & moved)
        return high & moved if n == 0 else jnp.bool_(n % 2)

    def each(h, n, sent, passed):
        if n > 1:
            if n % 2:
                sent(x_first, h, n)
                passed(x_first, y_second, h, n)
            else:
                sent(y_first, h, n)
                passed(y_first, x_second, h, n)
            return
        mine = goes_x_first(h, n, low, high)

        @pl.when(mine)
        def _():
            sent(x_first, h, n)
            passed(x_first, y_second, h, n)

        @pl.when(jnp.logical_not(mine))
        def _():
            sent(y_first, h, n)

        @pl.when(jnp.logical_not(goes_x_first(h, n, high, low)))
        def _():
            passed(y_first, x_second, h, n)

    def nothing(*_):
        pass

    def start(away, h, n):
        away(h, n).start()

    def forward(arrived, onward, h, n):
        arrived(h, n).wait_recv()
        onward(h, n).start()

    @pl.loop(0, heads)
    def _(h):
        load(h).wait()
        for n in range(CUTS):
            each(h, n, start, nothing)

    mask[...] = allowed_bias(lengths, lengths.shape[0], rows)

    @pl.loop(0, heads)
    def _(h):
        for n in range(CUTS):
            each(h, n, nothing, forward)

    g_copy.wait()

    @pl.loop(0, heads)
    def _(h):
        for n in range(CUTS):
            x_second(h, n).wait_recv()
        q = land[h, :, 0:size]
        k = land[h, :, size:2 * size]
        v = land[h, :, 2 * size:]
        g = g_all[:, pl.ds(pl.multiple_of(h * size, size), size)]
        for n, part in enumerate(head_grads(q, k, v, g, mask[...])):
            made[h, :, n * size:(n + 1) * size] = part.astype(made.dtype)
            bias_part[h, :, n * size:(n + 1) * size] = jnp.sum(part.reshape(-1, 8, size), axis=0)

    def bias_copy(n):
        return pltpu.make_async_remote_copy(
            src_ref=bias_all.at[me], dst_ref=bias_all.at[me], send_sem=bias_send.at[n],
            recv_sem=bias_recv.at[n], device_id={"dp": peers[n]}, device_id_type=MESH)

    for h in range(heads):
        bias_all[me, h:h + 1] = jnp.sum(bias_part[h], axis=0, keepdims=True)

    def sent_wait(away, h, n):
        away(h, n).wait_send()

    def passed_wait(arrived, onward, h, n):
        onward(h, n).wait_send()

    for n in range(len(peers)):
        bias_copy(n).start()

    @pl.loop(0, heads)
    def _(h):
        for n in range(CUTS):
            each(h, n, sent_wait, passed_wait)

    for n in range(len(peers)):
        bias_copy(n).wait()
    total = bias_all[0]
    for n in range(1, replicas):
        total = total + bias_all[n]
    total = total / replicas
    for h in range(heads):
        bias_out[h] = total[h:h + 1]


def solution(mesh):
    sections, replicas = mesh.shape["section"], mesh.shape["dp"]
    x_parts = 2
    shape = (sections, x_parts, sections // x_parts, replicas)

    def body(stash, grad_out, doc_lengths):
        _, _, rows, heads, width = stash.shape
        held = jnp.transpose(stash[0, 0], (1, 0, 2))
        pieces = heads * CUTS
        dma = pltpu.SemaphoreType.DMA
        made, bias = pl.pallas_call(
            functools.partial(kernel, shape),
            out_shape=(jax.ShapeDtypeStruct(held.shape, held.dtype),
                       jax.ShapeDtypeStruct((heads, 1, width), jnp.float32)),
            in_specs=[pl.BlockSpec(memory_space=pltpu.HBM), pl.BlockSpec(memory_space=pltpu.HBM),
                      pl.BlockSpec(memory_space=pltpu.SMEM)],
            out_specs=(pl.BlockSpec(memory_space=pltpu.VMEM), pl.BlockSpec(memory_space=pltpu.VMEM)),
            scratch_shapes=[
                pltpu.VMEM(held.shape, held.dtype),
                pltpu.VMEM(held.shape, held.dtype),
                pltpu.VMEM(held.shape, held.dtype),
                pltpu.VMEM(held.shape, held.dtype),
                pltpu.VMEM(grad_out.shape[2:], grad_out.dtype),
                pltpu.VMEM((rows, rows), jnp.float32),
                pltpu.VMEM((heads, 8, width), jnp.float32),
                pltpu.VMEM((replicas, heads, width), jnp.float32),
                *[dma((pieces,))] * 6,
                dma((heads,)), dma, dma((replicas - 1,)), dma((replicas - 1,)),
            ],
            compiler_params=pltpu.CompilerParams(
                collective_id=0, has_side_effects=True, vmem_limit_bytes=LIMIT),
            name="mirror_attention_grads",
        )(held, grad_out[0, 0], doc_lengths[0, 0])
        return jnp.transpose(made, (1, 0, 2))[None, None], jnp.transpose(bias, (1, 0, 2))

    in_specs = (
        P("section", "dp", None, "tp", None),
        P("section", "dp", None, "tp"),
        P("section", "dp", None),
    )
    out_specs = (P("section", "dp", None, "tp", None), P("section", "tp", None))
    return jax.shard_map(body, mesh=mesh, in_specs=in_specs, out_specs=out_specs, check_vma=False)
```

```python
import functools
import math

import jax
import jax.numpy as jnp
from jax import lax
from jax.experimental import pallas as pl
from jax.experimental.pallas import tpu as pltpu
from jax.sharding import PartitionSpec as P

MESH = pl.DeviceIdType.MESH
CUTS = 4
SHIFT = 1
LIMIT = 52 << 20


def partners(sections, x_parts, y_parts):
    section = lax.axis_index("section")
    x_hi, y = section // y_parts, section % y_parts
    over = (1 - x_hi) * y_parts + y
    flipped = x_hi * y_parts + (y_parts - 1 - y)
    return over, flipped


def allowed_bias(ends_ref, docs, rows):
    query = lax.broadcasted_iota(jnp.int32, (1, rows), 1)
    start = jnp.zeros((1, rows), jnp.int32)
    end = jnp.int32(0)
    for d in range(docs):
        end = end + ends_ref[d]
        start = jnp.where(query >= end, end, start)
    key = lax.broadcasted_iota(jnp.int32, (rows, rows), 0)
    query = lax.broadcasted_iota(jnp.int32, (rows, rows), 1)
    return jnp.where((key <= query) & (key >= start), 0.0, -jnp.inf).astype(jnp.float32)


def head_grads(q, k, v, g, mask):
    inv_root = 1.0 / math.sqrt(q.shape[-1])
    nt = (((1,), (1,)), ((), ()))
    tn = (((0,), (0,)), ((), ()))
    nn = (((1,), (0,)), ((), ()))
    dot = functools.partial(lax.dot_general, preferred_element_type=jnp.float32)
    scores = dot(k, q, nt) * (inv_root * math.log2(math.e)) + mask
    raised = jnp.exp2(scores - jnp.max(scores, axis=0, keepdims=True))
    prob = raised * (1.0 / jnp.sum(raised, axis=0, keepdims=True))
    prob_low = prob.astype(jnp.bfloat16)
    prob_grad = dot(v, g, nt)
    row_dot = jnp.sum(prob_low.astype(jnp.float32) * prob_grad, axis=0, keepdims=True)
    score_low = (prob * (prob_grad - row_dot) * inv_root).astype(jnp.bfloat16)
    return dot(score_low, k, tn), dot(score_low, q, nn), dot(prob_low, g, nn)


def kernel(shape, stash, grad_out, lengths, made, bias_out, own, from_over, from_flipped, land, g_all, mask,
           bias_part, bias_all, s1, r_over, r_flipped, s_over, s_flipped, r2, own_sem, g_sem, bias_send, bias_recv, ends, ends_sem):
    sections, x_parts, y_parts, replicas = shape
    heads, rows, width = land.shape
    size = width // 3
    cut = rows // CUTS
    over, flipped = partners(sections, x_parts, y_parts)
    me = lax.axis_index("dp")
    peers = [lax.rem(me + n, replicas) for n in range(1, replicas)]

    def load(h):
        return pltpu.make_async_copy(stash.at[h], own.at[h], own_sem.at[h])

    barrier = pltpu.get_barrier_semaphore()

    def greet(**to):
        pl.semaphore_signal(barrier, inc=1, device_id=to, device_id_type=MESH)

    greet(section=over)
    greet(section=flipped)

    for to in peers:
        greet(dp=to)

    @pl.loop(0, heads)
    def _(h):
        load(h).start()

    g_copy = pltpu.make_async_copy(grad_out, g_all, g_sem)
    g_copy.start()
    ends_copy = pltpu.make_async_copy(lengths, ends, ends_sem)
    ends_copy.start()
    pl.semaphore_wait(barrier, 2 + len(peers))

    def hop(src, dst, send, recv, h, n, to):
        at, rows_at = h * CUTS + n, pl.ds(n * cut, cut)
        return pltpu.make_async_remote_copy(
            src_ref=src.at[h, rows_at], dst_ref=dst.at[h, rows_at], send_sem=send.at[at],
            recv_sem=recv.at[at], device_id={"section": to}, device_id_type=MESH)

    def x_first(h, n):
        return hop(own, from_over, s1, r_over, h, n, over)

    def y_first(h, n):
        return hop(own, from_flipped, s1, r_flipped, h, n, flipped)

    def y_second(h, n):
        return hop(from_over, land, s_over, r2, h, n, flipped)

    def x_second(h, n):
        return hop(from_flipped, land, s_flipped, r2, h, n, over)

    y = lax.axis_index("section") % y_parts
    first_plane = lax.axis_index("tp") == 0
    low = first_plane & (y == 0)
    high = first_plane & (y == y_parts - 1)

    def goes_x_first(h, n, low, high):
        moved = h < SHIFT
        if n == 1:
            return jnp.logical_not(low & moved)
        return high & moved if n == 0 else jnp.bool_(n % 2)

    def each(h, n, sent, passed):
        if n > 1:
            if n % 2:
                sent(x_first, h, n)
                passed(x_first, y_second, h, n)
            else:
                sent(y_first, h, n)
                passed(y_first, x_second, h, n)
            return
        mine = goes_x_first(h, n, low, high)

        @pl.when(mine)
        def _():
            sent(x_first, h, n)
            passed(x_first, y_second, h, n)

        @pl.when(jnp.logical_not(mine))
        def _():
            sent(y_first, h, n)

        @pl.when(jnp.logical_not(goes_x_first(h, n, high, low)))
        def _():
            passed(y_first, x_second, h, n)

    def nothing(*_):
        pass

    def start(away, h, n):
        away(h, n).start()

    def forward(arrived, onward, h, n):
        arrived(h, n).wait_recv()
        onward(h, n).start()

    @pl.loop(0, heads)
    def _(h):
        load(h).wait()
        for n in range(CUTS):
            each(h, n, start, nothing)

    ends_copy.wait()
    mask[...] = allowed_bias(ends, ends.shape[0], rows)

    @pl.loop(0, heads)
    def _(h):
        for n in range(CUTS):
            each(h, n, nothing, forward)

    g_copy.wait()

    @pl.loop(0, heads)
    def _(h):
        for n in range(CUTS):
            x_second(h, n).wait_recv()
        q = land[h, :, 0:size]
        k = land[h, :, size:2 * size]
        v = land[h, :, 2 * size:]
        g = g_all[:, pl.ds(pl.multiple_of(h * size, size), size)]
        for n, part in enumerate(head_grads(q, k, v, g, mask[...])):
            made[h, :, n * size:(n + 1) * size] = part.astype(made.dtype)
            bias_part[h, :, n * size:(n + 1) * size] = jnp.sum(part.reshape(-1, 8, size), axis=0)

    def bias_copy(n):
        return pltpu.make_async_remote_copy(
            src_ref=bias_all.at[me], dst_ref=bias_all.at[me], send_sem=bias_send.at[n],
            recv_sem=bias_recv.at[n], device_id={"dp": peers[n]}, device_id_type=MESH)

    for h in range(heads):
        bias_all[me, h:h + 1] = jnp.sum(bias_part[h], axis=0, keepdims=True)

    def sent_wait(away, h, n):
        away(h, n).wait_send()

    def passed_wait(arrived, onward, h, n):
        onward(h, n).wait_send()

    for n in range(len(peers)):
        bias_copy(n).start()

    @pl.loop(0, heads)
    def _(h):
        for n in range(CUTS):
            each(h, n, sent_wait, passed_wait)

    for n in range(len(peers)):
        bias_copy(n).wait()
    total = bias_all[0]
    for n in range(1, replicas):
        total = total + bias_all[n]
    total = total / replicas
    for h in range(heads):
        bias_out[h] = total[h:h + 1]


def solution(mesh):
    sections, replicas = mesh.shape["section"], mesh.shape["dp"]
    x_parts = 2
    shape = (sections, x_parts, sections // x_parts, replicas)

    def body(stash, grad_out, doc_lengths):
        _, _, rows, heads, width = stash.shape
        held = jnp.transpose(stash[0, 0], (1, 0, 2))
        pieces = heads * CUTS
        dma = pltpu.SemaphoreType.DMA
        made, bias = pl.pallas_call(
            functools.partial(kernel, shape),
            out_shape=(jax.ShapeDtypeStruct(held.shape, held.dtype),
                       jax.ShapeDtypeStruct((heads, 1, width), jnp.float32)),
            in_specs=[pl.BlockSpec(memory_space=pltpu.HBM)] * 3,
            out_specs=(pl.BlockSpec(memory_space=pltpu.VMEM), pl.BlockSpec(memory_space=pltpu.VMEM)),
            scratch_shapes=[
                pltpu.VMEM(held.shape, held.dtype),
                pltpu.VMEM(held.shape, held.dtype),
                pltpu.VMEM(held.shape, held.dtype),
                pltpu.VMEM(held.shape, held.dtype),
                pltpu.VMEM(grad_out.shape[2:], grad_out.dtype),
                pltpu.VMEM((rows, rows), jnp.float32),
                pltpu.VMEM((heads, 8, width), jnp.float32),
                pltpu.VMEM((replicas, heads, width), jnp.float32),
                *[dma((pieces,))] * 6,
                dma((heads,)), dma, dma((replicas - 1,)), dma((replicas - 1,)),
                pltpu.SMEM(doc_lengths.shape[2:], doc_lengths.dtype), dma,
            ],
            compiler_params=pltpu.CompilerParams(
                collective_id=0, has_side_effects=True, vmem_limit_bytes=LIMIT),
            name="mirror_attention_grads",
        )(pltpu.with_memory_space_constraint(held, pltpu.HBM),
          pltpu.with_memory_space_constraint(grad_out[0, 0], pltpu.HBM),
          pltpu.with_memory_space_constraint(doc_lengths[0, 0], pltpu.HBM))
        return jnp.transpose(made, (1, 0, 2))[None, None], jnp.transpose(bias, (1, 0, 2))

    in_specs = (
        P("section", "dp", None, "tp", None),
        P("section", "dp", None, "tp"),
        P("section", "dp", None),
    )
    out_specs = (P("section", "dp", None, "tp", None), P("section", "tp", None))
    return jax.shard_map(body, mesh=mesh, in_specs=in_specs, out_specs=out_specs, check_vma=False)
```

```python
import functools
import math

import jax
import jax.numpy as jnp
from jax import lax
from jax.experimental import pallas as pl
from jax.experimental.pallas import tpu as pltpu
from jax.sharding import PartitionSpec as P

MESH = pl.DeviceIdType.MESH
CUTS = 2
SHIFT = 1
LIMIT = 52 << 20


def partners(sections, x_parts, y_parts):
    section = lax.axis_index("section")
    x_hi, y = section // y_parts, section % y_parts
    over = (1 - x_hi) * y_parts + y
    flipped = x_hi * y_parts + (y_parts - 1 - y)
    return over, flipped


def allowed_bias(ends_ref, docs, rows):
    query = lax.broadcasted_iota(jnp.int32, (1, rows), 1)
    start = jnp.zeros((1, rows), jnp.int32)
    end = jnp.int32(0)
    for d in range(docs):
        end = end + ends_ref[d]
        start = jnp.where(query >= end, end, start)
    key = lax.broadcasted_iota(jnp.int32, (rows, rows), 0)
    query = lax.broadcasted_iota(jnp.int32, (rows, rows), 1)
    return jnp.where((key <= query) & (key >= start), 0.0, -jnp.inf).astype(jnp.float32)


def head_grads(q, k, v, g, mask):
    inv_root = 1.0 / math.sqrt(q.shape[-1])
    nt = (((1,), (1,)), ((), ()))
    tn = (((0,), (0,)), ((), ()))
    nn = (((1,), (0,)), ((), ()))
    dot = functools.partial(lax.dot_general, preferred_element_type=jnp.float32)
    scores = dot(k, q, nt) * (inv_root * math.log2(math.e)) + mask
    raised = jnp.exp2(scores - jnp.max(scores, axis=0, keepdims=True))
    prob = raised * (1.0 / jnp.sum(raised, axis=0, keepdims=True))
    prob_low = prob.astype(jnp.bfloat16)
    prob_grad = dot(v, g, nt)
    row_dot = jnp.sum(prob_low.astype(jnp.float32) * prob_grad, axis=0, keepdims=True)
    score_low = (prob * (prob_grad - row_dot) * inv_root).astype(jnp.bfloat16)
    return dot(score_low, k, tn), dot(score_low, q, nn), dot(prob_low, g, nn)


def kernel(shape, stash, grad_out, lengths, made, bias_out, own, from_over, from_flipped, land, g_all, mask,
           bias_part, bias_all, s1, r_over, r_flipped, s_over, s_flipped, r2, own_sem, g_sem, bias_send, bias_recv, ends, ends_sem):
    sections, x_parts, y_parts, replicas = shape
    heads, rows, width = land.shape
    size = width // 3
    cut = rows // CUTS
    over, flipped = partners(sections, x_parts, y_parts)
    me = lax.axis_index("dp")
    peers = [lax.rem(me + n, replicas) for n in range(1, replicas)]

    def load(h):
        return pltpu.make_async_copy(stash.at[h], own.at[h], own_sem.at[h])

    barrier = pltpu.get_barrier_semaphore()

    def greet(**to):
        pl.semaphore_signal(barrier, inc=1, device_id=to, device_id_type=MESH)

    greet(section=over)
    greet(section=flipped)

    for to in peers:
        greet(dp=to)

    @pl.loop(0, heads)
    def _(h):
        load(h).start()

    g_copy = pltpu.make_async_copy(grad_out, g_all, g_sem)
    g_copy.start()
    ends_copy = pltpu.make_async_copy(lengths, ends, ends_sem)
    ends_copy.start()
    pl.semaphore_wait(barrier, 2 + len(peers))

    def hop(src, dst, send, recv, h, n, to):
        at, rows_at = h * CUTS + n, pl.ds(n * cut, cut)
        return pltpu.make_async_remote_copy(
            src_ref=src.at[h, rows_at], dst_ref=dst.at[h, rows_at], send_sem=send.at[at],
            recv_sem=recv.at[at], device_id={"section": to}, device_id_type=MESH)

    def x_first(h, n):
        return hop(own, from_over, s1, r_over, h, n, over)

    def y_first(h, n):
        return hop(own, from_flipped, s1, r_flipped, h, n, flipped)

    def y_second(h, n):
        return hop(from_over, land, s_over, r2, h, n, flipped)

    def x_second(h, n):
        return hop(from_flipped, land, s_flipped, r2, h, n, over)

    y = lax.axis_index("section") % y_parts
    first_plane = lax.axis_index("tp") == 0
    late = first_plane & (y == 0)
    mirror = first_plane & (y == y_parts - 1)

    def each(h, n, sent, passed):
        if n % 2:
            sent(x_first, h, n)
            passed(x_first, y_second, h, n)
            return
        moved = h < SHIFT

        @pl.when(mirror & moved)
        def _():
            sent(x_first, h, n)
            passed(x_first, y_second, h, n)

        @pl.when(jnp.logical_not(mirror & moved))
        def _():
            sent(y_first, h, n)

        @pl.when(jnp.logical_not(late & moved))
        def _():
            passed(y_first, x_second, h, n)

    def nothing(*_):
        pass

    def start(away, h, n):
        away(h, n).start()

    def forward(arrived, onward, h, n):
        arrived(h, n).wait_recv()
        onward(h, n).start()

    @pl.loop(0, heads)
    def _(h):
        load(h).wait()
        for n in range(CUTS):
            each(h, n, start, nothing)

    ends_copy.wait()
    mask[...] = allowed_bias(ends, ends.shape[0], rows)

    @pl.loop(0, heads)
    def _(h):
        for n in range(CUTS):
            each(h, n, nothing, forward)

    g_copy.wait()

    @pl.loop(0, heads)
    def _(h):
        for n in range(CUTS):
            x_second(h, n).wait_recv()
        q = land[h, :, 0:size]
        k = land[h, :, size:2 * size]
        v = land[h, :, 2 * size:]
        g = g_all[:, pl.ds(pl.multiple_of(h * size, size), size)]
        for n, part in enumerate(head_grads(q, k, v, g, mask[...])):
            made[h, :, n * size:(n + 1) * size] = part.astype(made.dtype)
            bias_part[h, :, n * size:(n + 1) * size] = jnp.sum(part.reshape(-1, 8, size), axis=0)

    def bias_copy(n):
        return pltpu.make_async_remote_copy(
            src_ref=bias_all.at[me], dst_ref=bias_all.at[me], send_sem=bias_send.at[n],
            recv_sem=bias_recv.at[n], device_id={"dp": peers[n]}, device_id_type=MESH)

    for h in range(heads):
        bias_all[me, h:h + 1] = jnp.sum(bias_part[h], axis=0, keepdims=True)

    def sent_wait(away, h, n):
        away(h, n).wait_send()

    def passed_wait(arrived, onward, h, n):
        onward(h, n).wait_send()

    for n in range(len(peers)):
        bias_copy(n).start()

    @pl.loop(0, heads)
    def _(h):
        for n in range(CUTS):
            each(h, n, sent_wait, passed_wait)

    for n in range(len(peers)):
        bias_copy(n).wait()
    total = bias_all[0]
    for n in range(1, replicas):
        total = total + bias_all[n]
    total = total / replicas
    for h in range(heads):
        bias_out[h] = total[h:h + 1]


def write_kernel(made, bias, made_out, bias_out, made_sem, bias_sem):
    copies = [pltpu.make_async_copy(bias, bias_out, bias_sem)]
    copies += [pltpu.make_async_copy(made.at[h], made_out.at[h], made_sem.at[h]) for h in range(made.shape[0])]
    for copy in copies:
        copy.start()
    for copy in copies:
        copy.wait()


def solution(mesh):
    sections, replicas = mesh.shape["section"], mesh.shape["dp"]
    x_parts = 2
    shape = (sections, x_parts, sections // x_parts, replicas)

    def body(stash, grad_out, doc_lengths):
        _, _, rows, heads, width = stash.shape
        held = jnp.transpose(stash[0, 0], (1, 0, 2))
        pieces = heads * CUTS
        dma = pltpu.SemaphoreType.DMA
        made, bias = pl.pallas_call(
            functools.partial(kernel, shape),
            out_shape=(jax.ShapeDtypeStruct(held.shape, held.dtype),
                       jax.ShapeDtypeStruct((heads, 1, width), jnp.float32)),
            in_specs=[pl.BlockSpec(memory_space=pltpu.HBM)] * 3,
            out_specs=(pl.BlockSpec(memory_space=pltpu.VMEM), pl.BlockSpec(memory_space=pltpu.VMEM)),
            scratch_shapes=[
                pltpu.VMEM(held.shape, held.dtype),
                pltpu.VMEM(held.shape, held.dtype),
                pltpu.VMEM(held.shape, held.dtype),
                pltpu.VMEM(held.shape, held.dtype),
                pltpu.VMEM(grad_out.shape[2:], grad_out.dtype),
                pltpu.VMEM((rows, rows), jnp.float32),
                pltpu.VMEM((heads, 8, width), jnp.float32),
                pltpu.VMEM((replicas, heads, width), jnp.float32),
                *[dma((pieces,))] * 6,
                dma((heads,)), dma, dma((replicas - 1,)), dma((replicas - 1,)),
                pltpu.SMEM(doc_lengths.shape[2:], doc_lengths.dtype), dma,
            ],
            compiler_params=pltpu.CompilerParams(
                collective_id=0, has_side_effects=True, vmem_limit_bytes=LIMIT),
            name="mirror_attention_grads",
        )(pltpu.with_memory_space_constraint(held, pltpu.HBM),
          pltpu.with_memory_space_constraint(grad_out[0, 0], pltpu.HBM),
          pltpu.with_memory_space_constraint(doc_lengths[0, 0], pltpu.HBM))
        made, bias = pl.pallas_call(
            write_kernel,
            out_shape=(jax.ShapeDtypeStruct(made.shape, made.dtype),
                       jax.ShapeDtypeStruct(bias.shape, bias.dtype)),
            in_specs=[pl.BlockSpec(memory_space=pltpu.VMEM)] * 2,
            out_specs=(pl.BlockSpec(memory_space=pltpu.HBM),) * 2,
            scratch_shapes=[dma((heads,)), dma],
            name="write_results",
        )(pltpu.with_memory_space_constraint(made, pltpu.VMEM),
          pltpu.with_memory_space_constraint(bias, pltpu.VMEM))
        return jnp.transpose(made, (1, 0, 2))[None, None], jnp.transpose(bias, (1, 0, 2))

    in_specs = (
        P("section", "dp", None, "tp", None),
        P("section", "dp", None, "tp"),
        P("section", "dp", None),
    )
    out_specs = (P("section", "dp", None, "tp", None), P("section", "tp", None))
    return jax.shard_map(body, mesh=mesh, in_specs=in_specs, out_specs=out_specs, check_vma=False)
```

```python
import functools
import math

import jax
import jax.numpy as jnp
from jax import lax
from jax.experimental import pallas as pl
from jax.experimental.pallas import tpu as pltpu
from jax.sharding import PartitionSpec as P

MESH = pl.DeviceIdType.MESH
CUTS = 2
SHIFT = 1
LIMIT = 52 << 20


def partners(sections, x_parts, y_parts):
    section = lax.axis_index("section")
    x_hi, y = section // y_parts, section % y_parts
    over = (1 - x_hi) * y_parts + y
    flipped = x_hi * y_parts + (y_parts - 1 - y)
    return over, flipped


def allowed_bias(ends_ref, docs, rows):
    query = lax.broadcasted_iota(jnp.int32, (1, rows), 1)
    start = jnp.zeros((1, rows), jnp.int32)
    end = jnp.int32(0)
    for d in range(docs):
        end = end + ends_ref[d]
        start = jnp.where(query >= end, end, start)
    key = lax.broadcasted_iota(jnp.int32, (rows, rows), 0)
    query = lax.broadcasted_iota(jnp.int32, (rows, rows), 1)
    return jnp.where((key <= query) & (key >= start), 0.0, -jnp.inf).astype(jnp.float32)


def head_grads(q, k, v, g, mask):
    inv_root = 1.0 / math.sqrt(q.shape[-1])
    nt = (((1,), (1,)), ((), ()))
    tn = (((0,), (0,)), ((), ()))
    nn = (((1,), (0,)), ((), ()))
    dot = functools.partial(lax.dot_general, preferred_element_type=jnp.float32)
    scores = dot(k, q, nt) * (inv_root * math.log2(math.e)) + mask
    raised = jnp.exp2(scores - jnp.max(scores, axis=0, keepdims=True))
    prob = raised * (1.0 / jnp.sum(raised, axis=0, keepdims=True))
    prob_low = prob.astype(jnp.bfloat16)
    prob_grad = dot(v, g, nt)
    row_dot = jnp.sum(prob_low.astype(jnp.float32) * prob_grad, axis=0, keepdims=True)
    score_low = (prob * (prob_grad - row_dot) * inv_root).astype(jnp.bfloat16)
    return dot(score_low, k, tn), dot(score_low, q, nn), dot(prob_low, g, nn)


def kernel(shape, stash, grad_out, lengths, made, bias_out, own, from_over, from_flipped, land, g_all, mask,
           bias_part, bias_all, s1, r_over, r_flipped, s_over, s_flipped, r2, own_sem, g_sem, bias_send, bias_recv, ends, ends_sem):
    sections, x_parts, y_parts, replicas = shape
    heads, rows, width = land.shape
    size = width // 3
    cut = rows // CUTS
    over, flipped = partners(sections, x_parts, y_parts)
    me = lax.axis_index("dp")
    peers = [lax.rem(me + n, replicas) for n in range(1, replicas)]

    def load(h):
        return pltpu.make_async_copy(stash.at[h], own.at[h], own_sem.at[h])

    barrier = pltpu.get_barrier_semaphore()

    def greet(**to):
        pl.semaphore_signal(barrier, inc=1, device_id=to, device_id_type=MESH)

    greet(section=over)
    greet(section=flipped)

    for to in peers:
        greet(dp=to)

    @pl.loop(0, heads)
    def _(h):
        load(h).start()

    g_copy = pltpu.make_async_copy(grad_out, g_all, g_sem)
    g_copy.start()
    ends_copy = pltpu.make_async_copy(lengths, ends, ends_sem)
    ends_copy.start()
    pl.semaphore_wait(barrier, 2 + len(peers))

    def hop(src, dst, send, recv, h, n, to):
        at, rows_at = h * CUTS + n, pl.ds(n * cut, cut)
        return pltpu.make_async_remote_copy(
            src_ref=src.at[h, rows_at], dst_ref=dst.at[h, rows_at], send_sem=send.at[at],
            recv_sem=recv.at[at], device_id={"section": to}, device_id_type=MESH)

    def x_first(h, n):
        return hop(own, from_over, s1, r_over, h, n, over)

    def y_first(h, n):
        return hop(own, from_flipped, s1, r_flipped, h, n, flipped)

    def y_second(h, n):
        return hop(from_over, land, s_over, r2, h, n, flipped)

    def x_second(h, n):
        return hop(from_flipped, land, s_flipped, r2, h, n, over)

    y = lax.axis_index("section") % y_parts
    first_plane = lax.axis_index("tp") == 0
    late = first_plane & (y == 0)
    mirror = first_plane & (y == y_parts - 1)

    def each(h, n, sent, passed):
        moved = (h < SHIFT) & (me % 2 == 1)
        if n % 2:
            @pl.when(jnp.logical_not(late & moved))
            def _():
                sent(x_first, h, n)
                passed(x_first, y_second, h, n)

            @pl.when(late & moved)
            def _():
                sent(y_first, h, n)

            @pl.when(mirror & moved)
            def _():
                passed(y_first, x_second, h, n)

            return

        @pl.when(mirror & moved)
        def _():
            sent(x_first, h, n)
            passed(x_first, y_second, h, n)

        @pl.when(jnp.logical_not(mirror & moved))
        def _():
            sent(y_first, h, n)

        @pl.when(jnp.logical_not(late & moved))
        def _():
            passed(y_first, x_second, h, n)

    def nothing(*_):
        pass

    def start(away, h, n):
        away(h, n).start()

    def forward(arrived, onward, h, n):
        arrived(h, n).wait_recv()
        onward(h, n).start()

    @pl.loop(0, heads)
    def _(h):
        load(h).wait()
        for n in range(CUTS):
            each(h, n, start, nothing)

    ends_copy.wait()
    mask[...] = allowed_bias(ends, ends.shape[0], rows)

    @pl.loop(0, heads)
    def _(h):
        for n in range(CUTS):
            each(h, n, nothing, forward)

    g_copy.wait()

    @pl.loop(0, heads)
    def _(h):
        for n in range(CUTS):
            x_second(h, n).wait_recv()
        q = land[h, :, 0:size]
        k = land[h, :, size:2 * size]
        v = land[h, :, 2 * size:]
        g = g_all[:, pl.ds(pl.multiple_of(h * size, size), size)]
        for n, part in enumerate(head_grads(q, k, v, g, mask[...])):
            made[h, :, n * size:(n + 1) * size] = part.astype(made.dtype)
            bias_part[h, :, n * size:(n + 1) * size] = jnp.sum(part.reshape(-1, 8, size), axis=0)

    def bias_copy(n):
        return pltpu.make_async_remote_copy(
            src_ref=bias_all.at[me], dst_ref=bias_all.at[me], send_sem=bias_send.at[n],
            recv_sem=bias_recv.at[n], device_id={"dp": peers[n]}, device_id_type=MESH)

    for h in range(heads):
        bias_all[me, h:h + 1] = jnp.sum(bias_part[h], axis=0, keepdims=True)

    def sent_wait(away, h, n):
        away(h, n).wait_send()

    def passed_wait(arrived, onward, h, n):
        onward(h, n).wait_send()

    for n in range(len(peers)):
        bias_copy(n).start()

    @pl.loop(0, heads)
    def _(h):
        for n in range(CUTS):
            each(h, n, sent_wait, passed_wait)

    for n in range(len(peers)):
        bias_copy(n).wait()
    total = bias_all[0]
    for n in range(1, replicas):
        total = total + bias_all[n]
    total = total / replicas
    for h in range(heads):
        bias_out[h] = total[h:h + 1]


def write_kernel(made, bias, made_out, bias_out, made_sem, bias_sem):
    copies = [pltpu.make_async_copy(bias, bias_out, bias_sem)]
    copies += [pltpu.make_async_copy(made.at[h], made_out.at[h], made_sem.at[h]) for h in range(made.shape[0])]
    for copy in copies:
        copy.start()
    for copy in copies:
        copy.wait()


def solution(mesh):
    sections, replicas = mesh.shape["section"], mesh.shape["dp"]
    x_parts = 2
    shape = (sections, x_parts, sections // x_parts, replicas)

    def body(stash, grad_out, doc_lengths):
        _, _, rows, heads, width = stash.shape
        held = jnp.transpose(stash[0, 0], (1, 0, 2))
        pieces = heads * CUTS
        dma = pltpu.SemaphoreType.DMA
        made, bias = pl.pallas_call(
            functools.partial(kernel, shape),
            out_shape=(jax.ShapeDtypeStruct(held.shape, held.dtype),
                       jax.ShapeDtypeStruct((heads, 1, width), jnp.float32)),
            in_specs=[pl.BlockSpec(memory_space=pltpu.HBM)] * 3,
            out_specs=(pl.BlockSpec(memory_space=pltpu.VMEM), pl.BlockSpec(memory_space=pltpu.VMEM)),
            scratch_shapes=[
                pltpu.VMEM(held.shape, held.dtype),
                pltpu.VMEM(held.shape, held.dtype),
                pltpu.VMEM(held.shape, held.dtype),
                pltpu.VMEM(held.shape, held.dtype),
                pltpu.VMEM(grad_out.shape[2:], grad_out.dtype),
                pltpu.VMEM((rows, rows), jnp.float32),
                pltpu.VMEM((heads, 8, width), jnp.float32),
                pltpu.VMEM((replicas, heads, width), jnp.float32),
                *[dma((pieces,))] * 6,
                dma((heads,)), dma, dma((replicas - 1,)), dma((replicas - 1,)),
                pltpu.SMEM(doc_lengths.shape[2:], doc_lengths.dtype), dma,
            ],
            compiler_params=pltpu.CompilerParams(
                collective_id=0, has_side_effects=True, vmem_limit_bytes=LIMIT),
            name="mirror_attention_grads",
        )(pltpu.with_memory_space_constraint(held, pltpu.HBM),
          pltpu.with_memory_space_constraint(grad_out[0, 0], pltpu.HBM),
          pltpu.with_memory_space_constraint(doc_lengths[0, 0], pltpu.HBM))
        made, bias = pl.pallas_call(
            write_kernel,
            out_shape=(jax.ShapeDtypeStruct(made.shape, made.dtype),
                       jax.ShapeDtypeStruct(bias.shape, bias.dtype)),
            in_specs=[pl.BlockSpec(memory_space=pltpu.VMEM)] * 2,
            out_specs=(pl.BlockSpec(memory_space=pltpu.HBM),) * 2,
            scratch_shapes=[dma((heads,)), dma],
            name="write_results",
        )(pltpu.with_memory_space_constraint(made, pltpu.VMEM),
          pltpu.with_memory_space_constraint(bias, pltpu.VMEM))
        return jnp.transpose(made, (1, 0, 2))[None, None], jnp.transpose(bias, (1, 0, 2))

    in_specs = (
        P("section", "dp", None, "tp", None),
        P("section", "dp", None, "tp"),
        P("section", "dp", None),
    )
    out_specs = (P("section", "dp", None, "tp", None), P("section", "tp", None))
    return jax.shard_map(body, mesh=mesh, in_specs=in_specs, out_specs=out_specs, check_vma=False)
```
